32 devices in a mesh: row: 8 (over y, x, core), col: 4 (over z).
Axes of the slice: x: 2, y: 2, z: 4, core: 2. Of those that a mesh axis runs over, the one named last changes fastest.
Arguments:
- anc_inverse: float32 [4096, 4096], P('row', 'col')
- off_factor: float32 [2, 4096, 4096], P(None, 'row', 'col'), may hold values from -0.09375 to 0.09375
- diag_inverse: float32 [2, 4096, 4096], P(None, 'row', 'col')
- block_mask: int32 [2, 32], P(None, 'row'), may hold values 0 or 1
- edge_child: int32 [2, 8192], P(None, ('row', 'col')), may hold values from 0 to 4095, as said below
- edge_other: int32 [2, 8192], P(None, ('row', 'col')), may hold values from 0 to 8191, as said below
Outputs:
- off_inverse: float32 [2, 4096, 4096], P(None, 'row', 'col')
- diag_part: float32 [2, 4096, 4096], P(None, 'row', 'col')
- resist: float32 [2, 8192], P(None, ('row', 'col'))
The draws below stay inside these ranges and needn't reach their ends.
Inputs may be any that keep to these rules, and one draw needn't show every extreme that they name: `edge_child`: edges come in runs of 256; run d, with c = d % 4, has u in [c * 4096 / 4, (c + 1) * 4096 / 4). `edge_other`: in run d of 256 edges, with r = d // 4, v lies in [r * 4096 / 8, (r + 1) * 4096 / 8) or in 4096 + [r * 4096 / 8, (r + 1) * 4096 / 8); v never equals u.
All inputs are finite; a program needn't handle non-finite values. No bound on the sum of `block_mask` on one device may be relied on, other than what follows from the above.
Results may differ from the reference program's by a relative error of at most 0.000073.
Values sent between devices are 32-bit elements; how exact they have to be, the bound alone decides.
No kernel may reach another device: no remote copies, remote signals or barrier semaphores. Data moves between devices by JAX's collectives and lax.ppermute only.
A program may use at most 128 MiB of HBM per device.

```python
import math
import jax
import jax.numpy as jnp
from jax import lax

ANCESTOR = 4096
SUPERCOLS = 4096
FRONTS = 2
BLOCK = 128
EDGE_DEV = 256
N_ROW = 8
N_COL = 4


def dominant(key, lead, order):
    key_off, key_diag = jax.random.split(key, 2)
    spread = jax.random.normal(key_off, (lead, order, order), jnp.float32)
    spread = (spread + jnp.swapaxes(spread, 1, 2)) * (0.5 / math.sqrt(order))
    diagonal = jnp.exp(jax.random.uniform(key_diag, (lead, order), jnp.float32, 0.0, math.log(4.0)))
    identity = jnp.eye(order, dtype=jnp.float32)
    return spread * (1.0 - identity) + identity * diagonal[:, None, :]


def draw_anc_inverse(key, part):
    return dominant(jax.random.fold_in(key, 11), 1, ANCESTOR)[0]


def draw_diag_inverse(key, part):
    return dominant(jax.random.fold_in(key, 13), FRONTS, SUPERCOLS)


def edge_pair(key):
    base = jax.random.fold_in(key, 29)
    key_u, key_kind, key_child, key_anc = jax.random.split(base, 4)
    total = EDGE_DEV * N_ROW * N_COL
    position = jnp.arange(total, dtype=jnp.int32)
    run_id = position // EDGE_DEV
    row_id = run_id // N_COL
    col_id = run_id % N_COL
    col_width = SUPERCOLS // N_COL
    row_width = SUPERCOLS // N_ROW
    anc_width = ANCESTOR // N_ROW
    shape = (FRONTS, total)
    near = col_id * col_width + jax.random.randint(key_u, shape, 0, col_width, dtype=jnp.int32)
    kind = jax.random.randint(key_kind, shape, 0, 2, dtype=jnp.int32)
    child_end = row_id * row_width + jax.random.randint(key_child, shape, 0, row_width, dtype=jnp.int32)
    child_end = jnp.where(child_end == near, row_id * row_width + (child_end - row_id * row_width + 1) % row_width, child_end)
    anc_end = SUPERCOLS + row_id * anc_width + jax.random.randint(key_anc, shape, 0, anc_width, dtype=jnp.int32)
    far = jnp.where(kind == 0, child_end, anc_end)
    return (near.astype(jnp.int32), far.astype(jnp.int32))


def draw_edge_child(key, part):
    return edge_pair(key)[0]


def draw_edge_other(key, part):
    return edge_pair(key)[1]


def set_ends(result, stream_key, least, high):
    index_at = [jax.random.randint(jax.random.fold_in(stream_key, axis), (), 0, length) for axis, length in enumerate(result.shape)]
    widest = result.shape.index(max(result.shape))
    neighbour = index_at[:widest] + [(index_at[widest] + 1) % result.shape[widest]] + index_at[widest + 1:]
    return result.at[tuple(index_at)].set(least).at[tuple(neighbour)].set(high)


def levels(key, shape, shards, least, top_value):
    level = 1.0
    for dim, shards_of in shards:
        steps = jax.random.uniform(jax.random.fold_in(jax.random.fold_in(key, 6), dim), (shards_of,), jnp.float32, least / len(shards), top_value / len(shards))
        level = level * jnp.repeat(jnp.exp(steps), shape[dim] // shards_of).reshape((-1,) + (1,) * (len(shape) - 1 - dim))
    return level


def centred(stream_key, shape, scale, limit, cuts=(), kind=jnp.bfloat16):
    level = levels(stream_key, shape, cuts, -0.22, 0.18) if cuts else 1.0
    entries = jax.random.normal(stream_key, shape, jnp.float32) * scale * level
    return jnp.minimum(jnp.maximum(entries, -limit), limit).astype(kind)


def setup_inputs(seed: int = 0) -> dict:
    splits = jax.random.split(jax.random.key(seed), 7)
    anc_inverse = draw_anc_inverse(jax.random.fold_in(splits[6], 71), 0)
    off_factor = centred(splits[1], (FRONTS, ANCESTOR, SUPERCOLS), ANCESTOR ** -0.5, 0.09375, ((1, 8), (2, 4)), jnp.float32)
    diag_inverse = draw_diag_inverse(jax.random.fold_in(splits[6], 71), 0)
    block_mask = set_ends((jax.random.randint(splits[3], (FRONTS, ANCESTOR // BLOCK), 0, 4) < 3).astype(jnp.int32), jax.random.fold_in(splits[3], 1), 0, 1)
    edge_child = draw_edge_child(jax.random.fold_in(splits[6], 71), 0)
    edge_other = draw_edge_other(jax.random.fold_in(splits[6], 71), 0)
    return {"anc_inverse": anc_inverse, "off_factor": off_factor, "diag_inverse": diag_inverse, "block_mask": block_mask, "edge_child": edge_child, "edge_other": edge_other}


def reference(anc_inverse, off_factor, diag_inverse, block_mask, edge_child, edge_other):
    keep = jnp.repeat(block_mask, BLOCK, axis=1).astype(jnp.float32)
    factor = off_factor * keep[:, :, None]
    off_inverse = -jnp.einsum("ab,kbi->kai", anc_inverse, factor, precision=lax.Precision.HIGHEST)
    diag_part = diag_inverse - jnp.einsum("kaj,kai->kji", off_inverse, factor, precision=lax.Precision.HIGHEST)
    cc_diag = jnp.diagonal(diag_part, axis1=1, axis2=2)
    z_diag = jnp.diagonal(anc_inverse)
    is_child = edge_other < SUPERCOLS
    child_v = jnp.clip(edge_other, 0, SUPERCOLS - 1).astype(jnp.int32)
    anc_v = jnp.clip(edge_other - SUPERCOLS, 0, ANCESTOR - 1).astype(jnp.int32)
    fronts = jnp.arange(FRONTS).astype(jnp.int32)[:, None]
    mixed = jnp.where(is_child, diag_part[fronts, child_v, edge_child], off_inverse[fronts, anc_v, edge_child])
    near = jnp.take_along_axis(cc_diag, edge_child, axis=1)
    far = jnp.where(is_child, jnp.take_along_axis(cc_diag, child_v, axis=1), z_diag[anc_v])
    resist = near + far - 2.0 * mixed
    return off_inverse, diag_part, resist
```

```python
import jax
import jax.numpy as jnp
from jax import lax
from jax.experimental import pallas as pl
from jax.experimental.pallas import tpu as pltpu
from jax.sharding import PartitionSpec as P


def assign_pairs(n_col, fronts):
    work = []
    for low in range(n_col):
        for high in range(low + 1, n_col):
            for front in range(fronts):
                middle = low + high - (n_col - 1)
                if high - low == 1:
                    middle = 0
                at_high = middle < 0 or (middle == 0 and front < fronts // 2)
                work.append((high, low, front) if at_high else (low, high, front))
    return work


def line_schedule(n_col, work, fronts, up):
    def fold(plane):
        return plane if up else n_col - 1 - plane

    wanted = {("z", src): n_col - 1 for src in range(n_col - 1)}
    for plane, partner, front in work:
        plane, partner = fold(plane), fold(partner)
        if partner < plane:
            wanted[(front, partner)] = max(wanted.get((front, partner), 0), plane)
    arrived = {key: {key[1]: 0} for key in wanted}
    rank = {"z": 0}
    for order, front in enumerate(range(fronts) if up else reversed(range(fronts))):
        rank[front] = 1 + order
    steps = []
    while True:
        sends = {}
        for plane in range(n_col - 1):
            ready = [
                key for key, last in wanted.items()
                if plane < last and plane in arrived[key] and plane + 1 not in arrived[key]
            ]
            if ready:
                sends[plane] = min(ready, key=lambda k: (k[0] != "z", -k[1] if k[0] == "z" else k[1], rank[k[0]]))
        if not sends:
            break
        steps.append(sends)
        for plane, key in sends.items():
            arrived[key][plane + 1] = len(steps)
    folded = [{fold(p): (k[0], fold(k[1])) for p, k in sends.items()} for sends in steps]
    where_at = {(k[0], fold(k[1])): {fold(p): s for p, s in at.items()} for k, at in arrived.items()}
    return folded, where_at


def color_slots(work, ready):
    slots = []
    load = [sum(it[0] == plane for it in work) for plane in range(1 + max(it[0] for it in work))]
    for item in sorted(work, key=lambda it: (ready[it], -load[it[0]], it)):
        for slot in slots:
            if all(other[0] != item[0] and other[1] != item[1] for other in slot):
                slot.append(item)
                break
        else:
            slots.append([item])
    return sorted(slots, key=lambda slot: max(ready[it] for it in slot))


def choose(index, options):
    groups = []
    for plane, array in options.items():
        for entry in groups:
            if entry[0] is array:
                entry[1].append(plane)
                break
        else:
            groups.append((array, [plane]))
    result = groups[0][0]
    for array, planes in groups[1:]:
        hit = index == planes[0]
        for plane in planes[1:]:
            hit = jnp.logical_or(hit, index == plane)
        result = jnp.where(hit, array, result)
    return result


def tie(value, after):
    return lax.optimization_barrier((value, after))[0]


def halve(part, axis, bit_axis, bit, n_row):
    mine = (lax.axis_index("row") >> bit_axis) & 1
    send = lax.dynamic_index_in_dim(part, 1 - mine, axis, keepdims=False)
    keep = lax.dynamic_index_in_dim(part, mine, axis, keepdims=False)
    return keep + lax.ppermute(send, "row", [(i, i ^ bit) for i in range(n_row)])


def reduce_scatter(part, n_row, groups):
    rows, width = part.shape
    bits = n_row.bit_length() - 1
    part = part.reshape((groups,) + (2,) * bits + (rows // groups // n_row, width))

    first = halve(part, bits, 0, 1, n_row)
    half = width // 2
    rest = list(range(1, bits))

    def run_rest(piece, order):
        left = list(reversed(rest))
        for bit in order:
            axis = 1 + left.index(bit)
            piece = halve(piece, axis, bit, 1 << bit, n_row)
            left.remove(bit)
        return piece

    one = run_rest(first[..., :half], rest)
    two = run_rest(first[..., half:], rest[::-1])
    return jnp.concatenate([one, two], axis=-1)


def per_device(anc_inverse, off_factor, diag_inverse, block_mask, edge_child, edge_other):
    fronts, anc_rows, col_width = off_factor.shape
    diag_rows = diag_inverse.shape[1]
    anc_cols = anc_inverse.shape[1]
    row_id = lax.axis_index("row")
    col_id = lax.axis_index("col")
    n_row, n_col = lax.axis_size("row"), lax.axis_size("col")
    groups = col_width // diag_rows
    supercols, ancestor = col_width * n_col, anc_cols * n_col
    high = lax.Precision.HIGH

    keep = jnp.repeat(block_mask, anc_rows // block_mask.shape[1], axis=1).astype(jnp.float32)
    factor = [off_factor[k] * keep[k][:, None] for k in range(fronts)]
    side_by_side = jnp.concatenate(factor, axis=1)
    columns = lax.all_gather(side_by_side, "row", axis=0, tiled=True)

    work = assign_pairs(n_col, fronts)
    plans = {up: line_schedule(n_col, work, fronts, up) for up in (True, False)}
    got = {up: {} for up in plans}
    spots = {up: plans[up][1] for up in plans}
    ready = {
        (plane, partner, front): spots[partner < plane][(front, partner)][plane] for plane, partner, front in work
    }

    def hop(number, after=()):
        earlier = tuple(got[up][number - 1] for up in got if number - 1 in got[up]) or (side_by_side,)
        for up, (steps, where_at) in plans.items():
            if number > len(steps):
                continue
            sends = steps[number - 1]
            options = {}
            for plane, (kind, src) in sends.items():
                if src == plane:
                    options[plane] = anc_inverse if kind == "z" else factor[kind]
                else:
                    options[plane] = got[up][where_at[(kind, src)][plane]]
            operand = choose(col_id, options)
            operand = tie(operand, earlier + tuple(after))
            step = 1 if up else -1
            got[up][number] = lax.ppermute(operand, "col", [(p, p + step) for p in sorted(sends)])

    for number in range(1, n_col):
        hop(number)
    whole_rows = jnp.zeros((anc_rows, ancestor), jnp.float32)
    whole_rows = lax.dynamic_update_slice_in_dim(whole_rows, anc_inverse, col_id * anc_cols, 1)
    for shift in range(1, n_col):
        options = {}
        for plane in range(n_col):
            src = (plane - shift) % n_col
            options[plane] = got[src < plane][spots[src < plane][("z", src)][plane]]
        block = choose(col_id, options)
        whole_rows = lax.dynamic_update_slice_in_dim(whole_rows, block, (col_id - shift) % n_col * anc_cols, 1)
    hop(n_col)
    off_cat = -jnp.dot(whole_rows, columns, precision=high)
    last = max(len(steps) for steps, where_at in plans.values())
    for number in range(n_col + 1, last + 1):
        hop(number, (off_cat,))
    off = [off_cat[:, k * col_width:(k + 1) * col_width] for k in range(fronts)]

    row_global = row_id * diag_rows + jnp.arange(diag_rows, dtype=jnp.int32)
    col_global = col_id * col_width + jnp.arange(col_width, dtype=jnp.int32)
    hit = row_global[:, None] == col_global[None, :]
    cc_part = jnp.stack([
        jnp.sum(jnp.where(hit, diag_inverse[k], 0.0), axis=0) - jnp.sum(off[k] * factor[k], axis=0)
        for k in range(fronts)
    ])
    cc_near = cc_part
    bit = 1
    while bit < n_row:
        cc_near = cc_near + lax.ppermute(cc_near, "row", [(i, i ^ bit) for i in range(n_row)])
        bit *= 2
    cc_rows = lax.dynamic_slice_in_dim(cc_near, row_id % groups * diag_rows, diag_rows, 1)
    cc_far = cc_rows
    for shift in range(1, n_col):
        pairs = []
        for row in range(n_row):
            owner = row // groups
            pairs.append((row * n_col + owner, row * n_col + (owner + shift) % n_col))
        came = lax.ppermute(cc_rows, ("row", "col"), pairs)
        cc_far = jnp.where((col_id - row_id // groups) % n_col == shift, came, cc_far)
    own = lax.dynamic_slice_in_dim(whole_rows, row_id * anc_rows, anc_rows, 1)
    eye = jnp.arange(anc_rows)[:, None] == jnp.arange(anc_rows)[None, :]
    z_far = jnp.sum(jnp.where(eye, own, 0.0), axis=0)

    off_inverse = jnp.stack(off)
    is_child = edge_other < supercols
    at_col = edge_child[:, :, None] == col_global
    at_row = edge_other[:, :, None] == row_global
    at_anc = edge_other[:, :, None] == supercols + row_id * anc_rows + jnp.arange(anc_rows, dtype=jnp.int32)

    def picked(at, values):
        return jnp.sum(jnp.where(at, values, 0.0), axis=-1)

    def mixed_of(at, block):
        rows = jnp.einsum("ker,krc->kec", at.astype(jnp.float32), block, precision=lax.Precision.HIGHEST)
        return picked(at_col, rows)

    ends = picked(at_col, cc_near[:, None, :]) + picked(at_row, cc_far[:, None, :]) + picked(at_anc, z_far)
    ends = ends - 2.0 * mixed_of(at_anc, off_inverse)

    def partial_sum(left, right):
        return lax.dot_general(left, right, (((0,), (0,)), ((), ())), precision=high)

    diag_piece = [reduce_scatter(partial_sum(factor[k], off[k]), n_row, groups) for k in range(fronts)]
    direct, turned = {}, {}
    done = list(diag_piece)
    slots = color_slots(work, ready)
    for place, slot in enumerate(slots):
        side = choose(col_id, {
            plane: got[partner < plane][spots[partner < plane][(front, partner)][plane]]
            for plane, partner, front in slot
        })
        mine = choose(col_id, {plane: off[front] for plane, partner, front in slot})
        if place == len(slots) - 1:
            side = tie(side, tuple(done[:-2]))
        piece = reduce_scatter(partial_sum(side, mine), n_row, groups)
        done.append(piece)
        sent = lax.ppermute(piece, "col", [(plane, partner) for plane, partner, front in slot])
        sent = jnp.stack([
            jnp.concatenate([sent[h][:, g * diag_rows:(g + 1) * diag_rows] for h in range(groups)], axis=1)
            for g in range(groups)
        ])
        for plane, partner, front in slot:
            direct[(plane, partner, front)] = piece
            turned[(partner, plane, front)] = sent

    block_id = row_id // groups
    parts = []
    for k in range(fronts):
        blocks = []
        for block in range(n_col):
            options = {}
            for plane in range(n_col):
                if plane == block:
                    options[plane] = diag_piece[k]
                elif (plane, block, k) in direct:
                    options[plane] = direct[(plane, block, k)]
                else:
                    options[plane] = turned[(plane, block, k)]
            blocks.append(choose(col_id, options))
        chunks = tie(jnp.stack(blocks), ends).reshape(n_row, -1, col_width)
        found = lax.all_to_all(chunks, "row", 0, 0, tiled=True).reshape(diag_rows, col_width)
        straight = jnp.zeros((), jnp.bool_)
        for plane in range(n_col):
            for block in range(n_col):
                if plane == block or (plane, block, k) in direct:
                    straight = jnp.logical_or(straight, jnp.logical_and(col_id == plane, block_id == block))
        parts.append(subtract_block(diag_inverse[k], found, straight))
    diag_part = jnp.stack(parts)
    resist = ends - 2.0 * mixed_of(at_row, diag_part)
    return (off_inverse, diag_part, resist)


def subtract_block(base, found, straight):
    rows, width = base.shape

    def kernel(flag, base_ref, found_ref, out_ref):
        @pl.when(flag[0] == 1)
        def _():
            out_ref[...] = base_ref[...] - found_ref[...]

        @pl.when(flag[0] == 0)
        def _():
            out_ref[...] = base_ref[...] - found_ref[...].T

    spec = pl.BlockSpec((rows, rows), lambda h, flag: (0, h))
    return pl.pallas_call(
        kernel,
        grid_spec=pltpu.PrefetchScalarGridSpec(
            num_scalar_prefetch=1, grid=(width // rows,), in_specs=[spec, spec], out_specs=spec
        ),
        out_shape=jax.ShapeDtypeStruct(base.shape, base.dtype),
        compiler_params=pltpu.CompilerParams(vmem_limit_bytes=32 * 1024 * 1024),
    )(straight.astype(jnp.int32).reshape(1), base, found)


def solution(mesh):
    placed = (
        P("row", "col"),
        P(None, "row", "col"),
        P(None, "row", "col"),
        P(None, "row"),
        P(None, ("row", "col")),
        P(None, ("row", "col")),
    )
    return jax.shard_map(
        per_device,
        mesh=mesh,
        in_specs=placed,
        out_specs=(P(None, "row", "col"), P(None, "row", "col"), P(None, ("row", "col"))),
        check_vma=False,
    )
```

```python
import functools

import jax
import jax.numpy as jnp
from jax import lax
from jax.experimental import pallas as pl
from jax.experimental.pallas import tpu as pltpu
from jax.sharding import PartitionSpec as P

SMALL = pl.CostEstimate(flops=0, bytes_accessed=0, transcendentals=0)


def assign_pairs(n_col, fronts):
    work = []
    for low in range(n_col):
        for high in range(low + 1, n_col):
            for front in range(fronts):
                middle = low + high - (n_col - 1)
                if high - low == 1:
                    middle = 0
                at_high = middle < 0 or (middle == 0 and front < fronts // 2)
                work.append((high, low, front) if at_high else (low, high, front))
    return work


def line_schedule(n_col, work, fronts, up):
    def fold(plane):
        return plane if up else n_col - 1 - plane

    wanted = {("z", src): n_col - 1 for src in range(n_col - 1)}
    for plane, partner, front in work:
        plane, partner = fold(plane), fold(partner)
        if partner < plane:
            wanted[(front, partner)] = max(wanted.get((front, partner), 0), plane)
    arrived = {key: {key[1]: 0} for key in wanted}
    rank = {"z": 0}
    for order, front in enumerate(range(fronts) if up else reversed(range(fronts))):
        rank[front] = 1 + order
    steps = []
    while True:
        sends = {}
        for plane in range(n_col - 1):
            ready = [
                key for key, last in wanted.items()
                if plane < last and plane in arrived[key] and plane + 1 not in arrived[key]
            ]
            if ready:
                sends[plane] = min(ready, key=lambda k: (k[0] != "z", -k[1] if k[0] == "z" else k[1], rank[k[0]]))
        if not sends:
            break
        steps.append(sends)
        for plane, key in sends.items():
            arrived[key][plane + 1] = len(steps)
    folded = [{fold(p): (k[0], fold(k[1])) for p, k in sends.items()} for sends in steps]
    where_at = {(k[0], fold(k[1])): {fold(p): s for p, s in at.items()} for k, at in arrived.items()}
    return folded, where_at


def color_slots(work, ready):
    slots = []
    load = [sum(it[0] == plane for it in work) for plane in range(1 + max(it[0] for it in work))]
    for item in sorted(work, key=lambda it: (ready[it], -load[it[0]], it)):
        for slot in slots:
            if all(other[0] != item[0] and other[1] != item[1] for other in slot):
                slot.append(item)
                break
        else:
            slots.append([item])
    return sorted(slots, key=lambda slot: max(ready[it] for it in slot))


def choose(index, options):
    groups = []
    for plane, array in options.items():
        for entry in groups:
            if entry[0] is array:
                entry[1].append(plane)
                break
        else:
            groups.append((array, [plane]))
    result = groups[0][0]
    for array, planes in groups[1:]:
        hit = index == planes[0]
        for plane in planes[1:]:
            hit = jnp.logical_or(hit, index == plane)
        result = jnp.where(hit, array, result)
    return result


def tie(value, after):
    return lax.optimization_barrier((value, after))[0]


def swap(part, axis, bit, n_row):
    mine = (lax.axis_index("row") >> bit) & 1
    send = lax.dynamic_index_in_dim(part, 1 - mine, axis, keepdims=False)
    keep = lax.dynamic_index_in_dim(part, mine, axis, keepdims=False)
    return keep + lax.ppermute(send, "row", [(i, i ^ (1 << bit)) for i in range(n_row)])


def reduce_scatter(halves, n_row, bits, after=None):
    other = [(i, i ^ 1) for i in range(n_row)]
    first = jnp.stack([kept + lax.ppermute(sent, "row", other) for kept, sent in halves])
    parts, groups, left_rows, rows, width = first.shape
    first = first.reshape((parts, groups) + (2,) * (bits - 1) + (rows, width))

    def run(piece, order):
        left = sorted(order, reverse=True)
        for bit in order:
            if after is not None and bit == order[-1]:
                piece = tie(piece, after)
            piece = swap(piece, 2 + left.index(bit), bit, n_row)
            left.remove(bit)
        return piece

    half = width // 2
    rest = list(range(1, bits))
    return first, jnp.concatenate([run(first[..., :half], rest), run(first[..., half:], rest[::-1])], axis=-1)


def split(value):
    upper = value.astype(jnp.bfloat16)
    return upper, (value - upper.astype(jnp.float32)).astype(jnp.bfloat16)


def three_pass(left, right, dims):
    (left_up, left_low), (right_up, right_low) = left, right
    dot = functools.partial(lax.dot_general, dimension_numbers=(dims, ((), ())), preferred_element_type=jnp.float32)
    return dot(left_up, right_up) + (dot(left_up, right_low) + dot(left_low, right_up))


def off_block(own, lower_blocks, upper_blocks, where, columns, factor):
    anc_rows, block = own.shape
    depth, width = columns.shape
    n_col = depth // block
    tile = min(256, width)

    def kernel(where, own_ref, *refs):
        lows, highs = refs[:n_col - 1], refs[n_col - 1:2 * n_col - 2]
        cols_ref, factor_ref, out_ref, sum_ref, diag_ref, upper, lower = refs[2 * n_col - 2:]
        hold, first = where[1], where[2]

        def take(shift, ref):
            upper[shift], lower[shift] = split(ref[...])

            @pl.when(lax.rem(where[0] - shift + n_col, n_col) == hold)
            def _():
                place = lax.broadcasted_iota(jnp.int32, ref.shape, 1) - lax.broadcasted_iota(jnp.int32, ref.shape, 0)
                diag_ref[...] = jnp.sum(jnp.where(place == first, ref[...], 0.0), axis=0, keepdims=True)

        @pl.when(pl.program_id(0) == 0)
        def _():
            take(0, own_ref)
            for shift in range(1, n_col):
                pl.when(where[0] >= shift)(functools.partial(take, shift, lows[shift - 1]))
                pl.when(where[0] < shift)(functools.partial(take, shift, highs[n_col - shift - 1]))

        total = jnp.zeros((anc_rows, tile), jnp.float32)
        for shift in range(n_col):
            at = lax.rem(where[0] - shift + n_col, n_col) * block
            right = split(cols_ref[pl.ds(pl.multiple_of(at, block), block), :])
            total -= three_pass((upper[shift], lower[shift]), right, ((1,), (0,)))
        out_ref[...] = total
        sum_ref[...] = -jnp.sum(total * factor_ref[...], axis=0, keepdims=True)

    whole = pl.BlockSpec((anc_rows, block), lambda n, where: (0, 0), pipeline_mode=pl.Buffered(1))
    return pl.pallas_call(
        kernel,
        grid_spec=pltpu.PrefetchScalarGridSpec(
            num_scalar_prefetch=1,
            grid=(width // tile,),
            in_specs=[whole] * (2 * n_col - 1) + [
                pl.BlockSpec((depth, tile), lambda n, where: (0, n)),
                pl.BlockSpec((anc_rows, tile), lambda n, where: (0, n)),
            ],
            out_specs=[
                pl.BlockSpec((anc_rows, tile), lambda n, where: (0, n)),
                pl.BlockSpec((1, tile), lambda n, where: (0, n)),
                pl.BlockSpec((1, block), lambda n, where: (0, 0)),
            ],
            scratch_shapes=[pltpu.VMEM((n_col, anc_rows, block), jnp.bfloat16)] * 2,
        ),
        out_shape=[
            jax.ShapeDtypeStruct((anc_rows, width), jnp.float32),
            jax.ShapeDtypeStruct((1, width), jnp.float32),
            jax.ShapeDtypeStruct((1, block), jnp.float32),
        ],
        compiler_params=pltpu.CompilerParams(vmem_limit_bytes=52 * 1024 * 1024),
        cost_estimate=pl.CostEstimate(
            flops=6 * anc_rows * depth * width, bytes_accessed=4 * (depth + 2 * anc_rows) * width, transcendentals=0
        ),
    )(where, own, *lower_blocks, *upper_blocks, columns, factor)


def partial_block(sides, which, off, front, mine, groups, bits):
    anc_rows, width = sides[0].shape
    tall = width // groups
    rows = tall >> bits

    def kernel(where, *refs):
        side_refs = refs[:len(sides)]
        off_ref, kept_ref, sent_ref, upper, lower, side_up, side_low = refs[len(sides):]

        @pl.when(pl.program_id(0) == 0)
        def _():
            upper[...], lower[...] = split(off_ref[...])

        def take(ref):
            side_up[...], side_low[...] = split(ref[...])

        for number, ref in enumerate(side_refs):
            pl.when(where[2] == number)(functools.partial(take, ref))
        found = three_pass((side_up[...], side_low[...]), (upper[...], lower[...]), ((0,), (0,)))
        found = found.reshape(1 << (bits - 1), 2, rows, width)
        zero = where[1] == 0
        kept_ref[0] = jnp.where(zero, found[:, 0], found[:, 1])
        sent_ref[0] = jnp.where(zero, found[:, 1], found[:, 0])

    out = jax.ShapeDtypeStruct((groups, 1 << (bits - 1), rows, width), jnp.float32)
    out_spec = pl.BlockSpec((1,) + out.shape[1:], lambda h, where: (h, 0, 0, 0))
    return pl.pallas_call(
        kernel,
        grid_spec=pltpu.PrefetchScalarGridSpec(
            num_scalar_prefetch=1,
            grid=(groups,),
            in_specs=[pl.BlockSpec((anc_rows, tall), lambda h, where: (0, h)) for _ in sides] + [
                pl.BlockSpec((anc_rows, width), lambda h, where: (0, where[0])),
            ],
            out_specs=[out_spec, out_spec],
            scratch_shapes=[pltpu.VMEM((anc_rows, width), jnp.bfloat16)] * 2
            + [pltpu.VMEM((anc_rows, tall), jnp.bfloat16)] * 2,
        ),
        out_shape=[out, out],
        compiler_params=pltpu.CompilerParams(vmem_limit_bytes=48 * 1024 * 1024),
        cost_estimate=SMALL,
    )(jnp.stack([front, mine, which]).astype(jnp.int32), *sides, off)


def subtract_blocks(base, found, straight):
    fronts, tall, width = base.shape
    n_row, _, rows, _ = found.shape

    def kernel(flag, base_ref, found_ref, out_ref):
        block = found_ref[...].reshape(tall, tall)

        @pl.when(flag[pl.program_id(0)] == 1)
        def _():
            out_ref[0] = base_ref[0] - block

        @pl.when(flag[pl.program_id(0)] == 0)
        def _():
            out_ref[0] = base_ref[0] - block.T

    spec = pl.BlockSpec((1, tall, tall), lambda k, h, flag: (k, 0, h))
    return pl.pallas_call(
        kernel,
        grid_spec=pltpu.PrefetchScalarGridSpec(
            num_scalar_prefetch=1,
            grid=(fronts, width // tall),
            in_specs=[spec, pl.BlockSpec((n_row, 1, rows, tall), lambda k, h, flag: (0, k, 0, h))],
            out_specs=spec,
        ),
        out_shape=jax.ShapeDtypeStruct(base.shape, base.dtype),
        compiler_params=pltpu.CompilerParams(vmem_limit_bytes=32 * 1024 * 1024),
    )(straight, base, found)


def per_device(anc_inverse, off_factor, diag_inverse, block_mask, edge_child, edge_other):
    fronts, anc_rows, col_width = off_factor.shape
    diag_rows = diag_inverse.shape[1]
    anc_cols = anc_inverse.shape[1]
    row_id = lax.axis_index("row")
    col_id = lax.axis_index("col")
    n_row, n_col = lax.axis_size("row"), lax.axis_size("col")
    groups = col_width // diag_rows
    supercols, ancestor = col_width * n_col, anc_cols * n_col

    keep = jnp.repeat(block_mask, anc_rows // block_mask.shape[1], axis=1).astype(jnp.float32)
    factor = [off_factor[k] * keep[k][:, None] for k in range(fronts)]
    side_by_side = jnp.concatenate(factor, axis=1)
    columns = lax.all_gather(side_by_side, "row", axis=0, tiled=True)

    work = assign_pairs(n_col, fronts)
    plans = {up: line_schedule(n_col, work, fronts, up) for up in (True, False)}
    got = {up: {} for up in plans}
    spots = {up: plans[up][1] for up in plans}
    ready = {
        (plane, partner, front): spots[partner < plane][(front, partner)][plane] for plane, partner, front in work
    }

    def hop(number, after=()):
        earlier = tuple(got[up][number - 1] for up in got if number - 1 in got[up]) or (side_by_side,)
        operands = {}
        for up, (steps, where_at) in plans.items():
            if number > len(steps):
                continue
            options = {}
            for plane, (kind, src) in steps[number - 1].items():
                if src == plane:
                    options[plane] = anc_inverse if kind == "z" else factor[kind]
                else:
                    options[plane] = got[up][where_at[(kind, src)][plane]]
            operands[up] = choose(col_id, options)
        operands = tie(operands, earlier + tuple(after))
        for up, operand in operands.items():
            step = 1 if up else -1
            sends = sorted(plans[up][0][number - 1])
            got[up][number] = lax.ppermute(operand, "col", [(p, p + step) for p in sends])

    for number in range(1, n_col):
        hop(number)
    hop(n_col)
    steps_of = {up: [got[up][step] for step in range(1, n_col)] for up in got}
    owner = row_id * anc_rows // anc_cols
    place = row_id * anc_rows - owner * anc_cols
    off, minus_sums, z_diag = off_block(
        anc_inverse, steps_of[True], steps_of[False], jnp.stack([col_id, owner, place]), columns, side_by_side
    )
    z_far = lax.dynamic_slice_in_dim(z_diag[0], place, anc_rows, 0)
    last = max(len(steps) for steps, where_at in plans.values())
    for number in range(n_col + 1, last + 1):
        hop(number, (off,))

    row_global = row_id * diag_rows + jnp.arange(diag_rows, dtype=jnp.int32)
    col_global = col_id * col_width + jnp.arange(col_width, dtype=jnp.int32)
    hit = row_global[:, None] == col_global[None, :]
    base_diag = jnp.sum(jnp.where(hit, diag_inverse, 0.0), axis=1)
    cc_part = base_diag + minus_sums.reshape(fronts, col_width)
    cc_near = cc_part
    bit = 1
    while bit < n_row:
        cc_near = cc_near + lax.ppermute(cc_near, "row", [(i, i ^ bit) for i in range(n_row)])
        bit *= 2
    cc_rows = lax.dynamic_slice_in_dim(cc_near, row_id % groups * diag_rows, diag_rows, 1)
    cc_far = cc_rows
    for shift in range(1, n_col):
        pairs = []
        for row in range(n_row):
            owner = row // groups
            pairs.append((row * n_col + owner, row * n_col + (owner + shift) % n_col))
        came = lax.ppermute(cc_rows, ("row", "col"), pairs)
        cc_far = jnp.where((col_id - row_id // groups) % n_col == shift, came, cc_far)
    is_child = edge_other < supercols
    at_col = edge_child[:, :, None] == col_global
    at_row = edge_other[:, :, None] == row_global
    at_anc = edge_other[:, :, None] == supercols + row_id * anc_rows + jnp.arange(anc_rows, dtype=jnp.int32)

    def picked(at, values):
        return jnp.sum(jnp.where(at, values, 0.0), axis=-1)

    def mixed_of(at, block):
        rows = jnp.einsum("ker,krc->kec", at.astype(jnp.float32), block, precision=lax.Precision.HIGHEST)
        return picked(at_col, rows)

    off_inverse = jnp.stack([off[:, k * col_width:(k + 1) * col_width] for k in range(fronts)])
    ends = picked(at_col, cc_near[:, None, :]) + picked(at_row, cc_far[:, None, :]) + picked(at_anc, z_far)
    ends = ends - 2.0 * mixed_of(at_anc, off_inverse)

    bits = n_row.bit_length() - 1
    low_bit = row_id & 1
    slots = color_slots(work, ready)
    no = jnp.int32(0)
    if n_col in got[True]:
        off = tie(off, (got[True][n_col], got[False][n_col]))
    halves = [partial_block([factor[k]], no, off, jnp.int32(k), low_bit, groups, bits) for k in range(fronts)]
    first, pieces = reduce_scatter(halves, n_row, bits)
    diag_piece = list(pieces)
    for up in got:
        for step in got[up]:
            if step > n_col:
                got[up][step] = tie(got[up][step], pieces)
    direct, turned = {}, {}
    came = None
    for start in range(0, len(slots), 2):
        halves = []
        for slot in slots[start:start + 2]:
            sides, which, fronts_of = [], {}, {}
            for plane, partner, front in slot:
                side = got[partner < plane][spots[partner < plane][(front, partner)][plane]]
                if not any(side is known for known in sides):
                    sides.append(side)
                which[plane] = [side is known for known in sides].index(True)
                fronts_of[plane] = front
            if slot is slots[1]:
                sides = list(tie(tuple(sides), first))
            table = [jnp.array([of.get(plane, 0) for plane in range(n_col)], jnp.int32)[col_id] for of in (which, fronts_of)]
            halves.append(partial_block(sides, table[0], off, table[1], low_bit, groups, bits))
        pieces = reduce_scatter(halves, n_row, bits, came)[1]
        moved = []
        for slot, piece in zip(slots[start:start + 2], pieces):
            sent = lax.ppermute(piece, "col", [(plane, partner) for plane, partner, front in slot])
            moved.append(sent)
            sent = jnp.stack([
                jnp.concatenate([sent[h][:, g * diag_rows:(g + 1) * diag_rows] for h in range(groups)], axis=1)
                for g in range(groups)
            ])
            for plane, partner, front in slot:
                direct[(plane, partner, front)] = piece
                turned[(partner, plane, front)] = sent
        came = tuple(moved)

    block_id = row_id // groups
    chunks = []
    straight = []
    for k in range(fronts):
        blocks = []
        for block in range(n_col):
            options = {}
            for plane in range(n_col):
                if plane == block:
                    options[plane] = diag_piece[k]
                elif (plane, block, k) in direct:
                    options[plane] = direct[(plane, block, k)]
                else:
                    options[plane] = turned[(plane, block, k)]
            blocks.append(choose(col_id, options))
        chunks.append(jnp.stack(blocks).reshape(n_row, -1, col_width))
        flag = jnp.zeros((), jnp.bool_)
        for plane in range(n_col):
            for block in range(n_col):
                if plane == block or (plane, block, k) in direct:
                    flag = jnp.logical_or(flag, jnp.logical_and(col_id == plane, block_id == block))
        straight.append(flag)
    chunks = tie(jnp.stack(chunks, axis=1), ends)
    found = lax.all_to_all(chunks, "row", 0, 0, tiled=True)
    diag_part = subtract_blocks(diag_inverse, found, jnp.stack(straight).astype(jnp.int32))
    resist = ends - 2.0 * mixed_of(at_row, diag_part)
    return (off_inverse, diag_part, resist)


def solution(mesh):
    placed = (
        P("row", "col"),
        P(None, "row", "col"),
        P(None, "row", "col"),
        P(None, "row"),
        P(None, ("row", "col")),
        P(None, ("row", "col")),
    )
    return jax.shard_map(
        per_device,
        mesh=mesh,
        in_specs=placed,
        out_specs=(P(None, "row", "col"), P(None, "row", "col"), P(None, ("row", "col"))),
        check_vma=False,
    )
```

```python
import functools

import jax
import jax.numpy as jnp
from jax import lax
from jax.experimental import pallas as pl
from jax.experimental.pallas import tpu as pltpu
from jax.sharding import PartitionSpec as P

SMALL = pl.CostEstimate(flops=1, bytes_accessed=1, transcendentals=0)


def assign_pairs(n_col, fronts):
    work = []
    for low in range(n_col):
        for high in range(low + 1, n_col):
            for front in range(fronts):
                middle = low + high - (n_col - 1)
                if high - low == 1:
                    middle = 0
                at_high = middle < 0 or (middle == 0 and front < fronts // 2)
                work.append((high, low, front) if at_high else (low, high, front))
    return work


def line_schedule(n_col, work, fronts, up):
    def fold(plane):
        return plane if up else n_col - 1 - plane

    wanted = {("z", src): n_col - 1 for src in range(n_col - 1)}
    for plane, partner, front in work:
        plane, partner = fold(plane), fold(partner)
        if partner < plane:
            wanted[(front, partner)] = max(wanted.get((front, partner), 0), plane)
    arrived = {key: {key[1]: 0} for key in wanted}
    rank = {"z": 0}
    for front in range(fronts):
        rank[front] = 1 + front
    steps = []
    while True:
        sends = {}
        for plane in range(n_col - 1):
            ready = [
                key for key, last in wanted.items()
                if plane < last and plane in arrived[key] and plane + 1 not in arrived[key]
            ]
            if ready:
                sends[plane] = min(ready, key=lambda k: (k[0] != "z", -k[1] if k[0] == "z" else k[1], rank[k[0]]))
        if not sends:
            break
        steps.append(sends)
        for plane, key in sends.items():
            arrived[key][plane + 1] = len(steps)
    folded = [{fold(p): (k[0], fold(k[1])) for p, k in sends.items()} for sends in steps]
    where_at = {(k[0], fold(k[1])): {fold(p): s for p, s in at.items()} for k, at in arrived.items()}
    return folded, where_at


def color_slots(work, ready):
    slots = []
    load = [sum(it[0] == plane for it in work) for plane in range(1 + max(it[0] for it in work))]
    for item in sorted(work, key=lambda it: (ready[it], -load[it[0]], it)):
        for slot in slots:
            if all(other[0] != item[0] and other[1] != item[1] for other in slot):
                slot.append(item)
                break
        else:
            slots.append([item])
    return sorted(slots, key=lambda slot: max(ready[it] for it in slot))


def choose(index, options):
    groups = []
    for plane, array in options.items():
        for entry in groups:
            if entry[0] is array:
                entry[1].append(plane)
                break
        else:
            groups.append((array, [plane]))
    result = groups[0][0]
    for array, planes in groups[1:]:
        hit = index == planes[0]
        for plane in planes[1:]:
            hit = jnp.logical_or(hit, index == plane)
        result = jnp.where(hit, array, result)
    return result


ANYWHERE = pl.BlockSpec(memory_space=pl.ANY)


def tie(values, after):
    values, after = tuple(values), tuple(after)

    def kernel(*refs):
        del refs

    return pl.pallas_call(
        kernel,
        in_specs=[ANYWHERE] * (len(values) + len(after)),
        out_specs=[ANYWHERE] * len(values),
        out_shape=[jax.ShapeDtypeStruct(value.shape, value.dtype) for value in values],
        input_output_aliases={at: at for at in range(len(values))},
        cost_estimate=SMALL,
    )(*values, *after)


def pick(index, options, after=()):
    arrays, number = [], {}
    for plane, array in options.items():
        if not any(array is other for other in arrays):
            arrays.append(array)
        number[plane] = [array is other for other in arrays].index(True)
    table = jnp.array([number.get(plane, 0) for plane in range(1 + max(number))], jnp.int32)
    which = table[jnp.minimum(index, max(number))]

    rows, width = arrays[0].shape
    parts = 4

    def kernel(which, *refs):
        out_ref = refs[-1]
        for at in range(len(arrays)):
            @pl.when(which[0] == at)
            def _():
                out_ref[...] = refs[at][...]

    spec = pl.BlockSpec((rows // parts, width), lambda n, which: (n, 0))
    return pl.pallas_call(
        kernel,
        grid_spec=pltpu.PrefetchScalarGridSpec(
            num_scalar_prefetch=1,
            grid=(parts,),
            in_specs=[spec] * len(arrays) + [ANYWHERE] * len(after),
            out_specs=spec,
        ),
        out_shape=jax.ShapeDtypeStruct(arrays[0].shape, arrays[0].dtype),
        cost_estimate=pl.CostEstimate(flops=0, bytes_accessed=2 * 4 * arrays[0].size, transcendentals=0),
    )(which.astype(jnp.int32).reshape(1), *arrays, *after)


def split(value):
    upper = value.astype(jnp.bfloat16)
    return upper, (value - upper.astype(jnp.float32)).astype(jnp.bfloat16)


def three_pass(left, right, dims):
    (left_up, left_low), (right_up, right_low) = left, right
    dot = functools.partial(lax.dot_general, dimension_numbers=(dims, ((), ())), preferred_element_type=jnp.float32)
    return dot(left_up, right_up) + (dot(left_up, right_low) + dot(left_low, right_up))


def off_block(blocks, where, columns, begun=None, factor=None, after=()):
    shifts = sorted(blocks)
    refs_of = {shift: len(blocks[shift]) for shift in shifts}
    anc_rows, block = blocks[shifts[0]][0].shape
    depth, width = columns.shape
    n_col = depth // block
    tile = min(256, width)
    last = factor is not None

    def kernel(where, *refs):
        refs = list(refs)
        held = {shift: [refs.pop(0) for _ in range(refs_of[shift])] for shift in shifts}
        cols_ref = refs.pop(0)
        begun_ref = refs.pop(0) if begun is not None else None
        factor_ref = refs.pop(0) if last else None
        del refs[:len(after)]
        out_ref = refs.pop(0)
        sum_ref, diag_ref = (refs.pop(0), refs.pop(0)) if last else (None, None)
        upper, lower = refs
        hold, first = where[1], where[2]

        def take(at, shift, ref):
            upper[at], lower[at] = split(ref[...])
            if last:
                @pl.when(lax.rem(where[0] - shift + n_col, n_col) == hold)
                def _():
                    place = lax.broadcasted_iota(jnp.int32, ref.shape, 1) - lax.broadcasted_iota(jnp.int32, ref.shape, 0)
                    diag_ref[...] = jnp.sum(jnp.where(place == first, ref[...], 0.0), axis=0, keepdims=True)

        @pl.when(pl.program_id(0) == 0)
        def _():
            if last:
                diag_ref[...] = jnp.zeros_like(diag_ref)
            for at, shift in enumerate(shifts):
                if shift == 0:
                    take(at, shift, held[shift][0])
                else:
                    pl.when(where[0] >= shift)(functools.partial(take, at, shift, held[shift][0]))
                    pl.when(where[0] < shift)(functools.partial(take, at, shift, held[shift][1]))

        total = jnp.zeros((anc_rows, tile), jnp.float32) if begun is None else begun_ref[...]
        for at, shift in enumerate(shifts):
            start = lax.rem(where[0] - shift + n_col, n_col) * block
            right = split(cols_ref[pl.ds(pl.multiple_of(start, block), block), :])
            total -= three_pass((upper[at], lower[at]), right, ((1,), (0,)))
        out_ref[...] = total
        if last:
            sum_ref[...] = -jnp.sum(total * factor_ref[...], axis=0, keepdims=True)

    whole = pl.BlockSpec((anc_rows, block), lambda n, where: (0, 0), pipeline_mode=pl.Buffered(1))
    tall = pl.BlockSpec((anc_rows, tile), lambda n, where: (0, n))
    args = [array for shift in shifts for array in blocks[shift]] + [columns]
    in_specs = [whole] * (len(args) - 1) + [pl.BlockSpec((depth, tile), lambda n, where: (0, n))]
    for extra in (begun, factor):
        if extra is not None:
            args.append(extra)
            in_specs.append(tall)
    args += after
    in_specs += [ANYWHERE] * len(after)
    out_specs, out_shape = [tall], [jax.ShapeDtypeStruct((anc_rows, width), jnp.float32)]
    if last:
        out_specs += [
            pl.BlockSpec((1, tile), lambda n, where: (0, n)), pl.BlockSpec((1, block), lambda n, where: (0, 0))
        ]
        out_shape += [
            jax.ShapeDtypeStruct((1, width), jnp.float32), jax.ShapeDtypeStruct((1, block), jnp.float32)
        ]
    return pl.pallas_call(
        kernel,
        grid_spec=pltpu.PrefetchScalarGridSpec(
            num_scalar_prefetch=1,
            grid=(width // tile,),
            in_specs=in_specs,
            out_specs=out_specs,
            scratch_shapes=[pltpu.VMEM((len(shifts), anc_rows, block), jnp.bfloat16)] * 2,
        ),
        out_shape=out_shape,
        compiler_params=pltpu.CompilerParams(vmem_limit_bytes=52 * 1024 * 1024),
        cost_estimate=pl.CostEstimate(
            flops=6 * anc_rows * len(shifts) * block * width, bytes_accessed=4 * depth * width, transcendentals=0
        ),
    )(where, *args)


def halves_of(block, low, high, a_refs, b_refs):
    many, rows, width = block.shape
    half = width // 2
    left = block[..., :half].reshape(many // 2, 2, rows, half)
    right = block[..., half:].reshape(2, many // 2, rows, half)
    a_refs[0][0, 0] = jnp.where(low == 0, left[:, 0], left[:, 1])
    a_refs[1][0, 0] = jnp.where(low == 0, left[:, 1], left[:, 0])
    b_refs[0][0, 0] = jnp.where(high == 0, right[0], right[1])
    b_refs[1][0, 0] = jnp.where(high == 0, right[1], right[0])


def partial_blocks(sides, mates, which, row_id, width, groups, bits, after=()):
    anc_rows = mates[0][0].shape[0]
    part = width // groups // 2
    many = 1 << (bits - 1)
    rows = part // many
    count = len(sides)

    def kernel(where, *refs):
        side_refs = [refs[2 * at:2 * at + 2] for at in range(count)]
        refs = refs[2 * count:]
        mate_refs = [refs[2 * at:2 * at + 2] for at in range(len(mates))]
        keep_a, send_a, keep_b, send_b, upper, lower, side_up, side_low = refs[2 * len(mates) + len(after):]
        this = pl.program_id(0)

        def take_side(pair):
            for core in range(2):
                side_up[core], side_low[core] = split(pair[core][...])

        def take_mate(pair):
            for core in range(2):
                upper[core], lower[core] = split(pair[core][...])

        for at in range(count):
            pl.when(this == at)(functools.partial(take_side, side_refs[at]))

        @pl.when(pl.program_id(1) == 0)
        def _():
            for at in range(count):
                for number in range(len(mates)):
                    pl.when(jnp.logical_and(this == at, where[3 + 2 * count + at] == number))(
                        functools.partial(take_mate, mate_refs[number])
                    )

        found = jnp.zeros((part, width), jnp.float32)
        for core in range(2):
            found += three_pass((side_up[core], side_low[core]), (upper[core], lower[core]), ((0,), (0,)))
        halves_of(found.reshape(many, rows, width), where[1], where[2], (keep_a, send_a), (keep_b, send_b))

    def side_spec(at):
        first = 2 * groups * sides[at // 2][4]
        return pl.BlockSpec((anc_rows, part), lambda n, h, where: (where[3 + at], first + 2 * h + where[0]))

    def mate_spec(front):
        return pl.BlockSpec((anc_rows, width), lambda n, h, where: (0, front), pipeline_mode=pl.Buffered(1))

    out = jax.ShapeDtypeStruct((count, groups, many // 2, rows, width // 2), jnp.float32)
    out_spec = pl.BlockSpec((1, 1) + out.shape[2:], lambda n, h, where: (n, h, 0, 0, 0))
    scalars = [row_id & 1, (row_id >> 1) & 1, (row_id >> (bits - 1)) & 1]
    for own, own_at, other, other_at, front in sides:
        scalars += [own_at, other_at]
    return pl.pallas_call(
        kernel,
        grid_spec=pltpu.PrefetchScalarGridSpec(
            num_scalar_prefetch=1,
            grid=(count, groups),
            in_specs=[side_spec(at) for at in range(2 * count)]
            + [mate_spec(front) for own, other, front in mates for core in range(2)]
            + [ANYWHERE] * len(after),
            out_specs=[out_spec] * 4,
            scratch_shapes=[pltpu.VMEM((2, anc_rows, width), jnp.bfloat16)] * 2
            + [pltpu.VMEM((2, anc_rows, part), jnp.bfloat16)] * 2,
        ),
        out_shape=[out] * 4,
        compiler_params=pltpu.CompilerParams(vmem_limit_bytes=48 * 1024 * 1024),
        cost_estimate=pl.CostEstimate(
            flops=2 * count * anc_rows * width * width, bytes_accessed=count * width * width, transcendentals=0
        ),
    )(
        jnp.stack(scalars + which).astype(jnp.int32),
        *[array for own, own_at, other, other_at, front in sides for array in (own, other)],
        *[array for own, other, front in mates for array in (own, other)],
        *after,
    )


def add_split(keep_a, came_a, keep_b, came_b, low, high):
    count, groups, many, rows, half = keep_a.shape

    def kernel(where, ka, ca, kb, cb, keep_a, send_a, keep_b, send_b):
        block = jnp.concatenate([ka[0, 0] + ca[0, 0], kb[0, 0] + cb[0, 0]], axis=-1)
        halves_of(block, where[0], where[1], (keep_a, send_a), (keep_b, send_b))

    spec = pl.BlockSpec((1, 1, many, rows, half), lambda n, h, where: (n, h, 0, 0, 0))
    out = jax.ShapeDtypeStruct((count, groups, many // 2, rows, half), jnp.float32)
    out_spec = pl.BlockSpec((1, 1) + out.shape[2:], lambda n, h, where: (n, h, 0, 0, 0))
    return pl.pallas_call(
        kernel,
        grid_spec=pltpu.PrefetchScalarGridSpec(
            num_scalar_prefetch=1, grid=(count, groups), in_specs=[spec] * 4, out_specs=[out_spec] * 4
        ),
        out_shape=[out] * 4,
        cost_estimate=pl.CostEstimate(flops=keep_a.size, bytes_accessed=4 * keep_a.size, transcendentals=0),
    )(jnp.stack([low, high]).astype(jnp.int32), keep_a, came_a, keep_b, came_b)


def add_chips(halves, row_id, n_row, bits):
    for step in range(1, bits):
        keep_a, send_a, keep_b, send_b = halves
        low, high = step, bits - step
        came_a = lax.ppermute(send_a, "row", [(i, i ^ (1 << low)) for i in range(n_row)])
        came_b = lax.ppermute(send_b, "row", [(i, i ^ (1 << high)) for i in range(n_row)])
        if step < bits - 1:
            halves = add_split(keep_a, came_a, keep_b, came_b, (row_id >> (low + 1)) & 1, (row_id >> (high - 1)) & 1)
    found = jnp.concatenate([keep_a + came_a, keep_b + came_b], axis=-1)
    return found.reshape(found.shape[:2] + found.shape[3:])


def subtract_blocks(base, found, straight):
    fronts, tall, width = base.shape
    n_row, _, rows, _ = found.shape

    def kernel(flag, base_ref, found_ref, out_ref):
        cores = found_ref[...].reshape(n_row // 2, 2, rows, tall)
        block = jnp.concatenate([cores[:, core].reshape(tall // 2, tall) for core in range(2)], axis=0)

        @pl.when(flag[pl.program_id(0)] == 1)
        def _():
            out_ref[0] = base_ref[0] - block

        @pl.when(flag[pl.program_id(0)] == 0)
        def _():
            out_ref[0] = base_ref[0] - block.T

    spec = pl.BlockSpec((1, tall, tall), lambda k, h, flag: (k, 0, h))
    return pl.pallas_call(
        kernel,
        grid_spec=pltpu.PrefetchScalarGridSpec(
            num_scalar_prefetch=1,
            grid=(fronts, width // tall),
            in_specs=[spec, pl.BlockSpec((n_row, 1, rows, tall), lambda k, h, flag: (0, k, 0, h))],
            out_specs=spec,
        ),
        out_shape=jax.ShapeDtypeStruct(base.shape, base.dtype),
        compiler_params=pltpu.CompilerParams(vmem_limit_bytes=32 * 1024 * 1024),
    )(straight, base, found)


def per_device(anc_inverse, off_factor, diag_inverse, block_mask, edge_child, edge_other):
    fronts, anc_rows, col_width = off_factor.shape
    diag_rows = diag_inverse.shape[1]
    anc_cols = anc_inverse.shape[1]
    row_id = lax.axis_index("row")
    col_id = lax.axis_index("col")
    n_row, n_col = lax.axis_size("row"), lax.axis_size("col")
    groups = col_width // diag_rows
    supercols, ancestor = col_width * n_col, anc_cols * n_col

    keep = jnp.repeat(block_mask, anc_rows // block_mask.shape[1], axis=1).astype(jnp.float32)
    factor = [off_factor[k] * keep[k][:, None] for k in range(fronts)]
    side_by_side = jnp.concatenate(factor, axis=1)
    columns = lax.all_gather(side_by_side, "row", axis=0, tiled=True)

    work = assign_pairs(n_col, fronts)
    plans = {up: line_schedule(n_col, work, fronts, up) for up in (True, False)}
    got = {up: {} for up in plans}
    spots = {up: plans[up][1] for up in plans}
    ready = {
        (plane, partner, front): spots[partner < plane][(front, partner)][plane] for plane, partner, front in work
    }

    def hop(number, after=()):
        operands = {}
        for up, (steps, where_at) in plans.items():
            if number > len(steps):
                continue
            options = {}
            for plane, (kind, src) in steps[number - 1].items():
                if src == plane:
                    options[plane] = anc_inverse if kind == "z" else factor[kind]
                else:
                    options[plane] = got[up][where_at[(kind, src)][plane]]
            operands[up] = choose(col_id, options)
        earlier = tuple(got[up][number - 1] for up in got if number - 1 in got[up]) or tuple(factor)
        operands = dict(zip(operands, tie(operands.values(), earlier + after)))
        for up, operand in operands.items():
            step = 1 if up else -1
            sends = sorted(plans[up][0][number - 1])
            got[up][number] = lax.ppermute(operand, "col", [(p, p + step) for p in sends])

    owner = row_id * anc_rows // anc_cols
    place = row_id * anc_rows - owner * anc_cols
    where = jnp.stack([col_id, owner, place])
    for number in range(1, n_col + 1):
        hop(number)
    blocks = {0: [anc_inverse]}
    for shift in range(1, n_col):
        blocks[shift] = [got[True][shift], got[False][n_col - shift]]
    off, sums, z_diag = off_block(blocks, where, columns, None, side_by_side)
    bits = n_row.bit_length() - 1
    to_core = [(i, i ^ 1) for i in range(n_row)]
    off_other = lax.ppermute(off, "row", to_core)
    last = max(len(steps) for steps, where_at in plans.values())
    for step in range(n_col + 1, last + 1):
        hop(step)
    slots = color_slots(work, ready)
    slot_jobs = [("slot", number) for number in range(len(slots))]
    early = slot_jobs[:1] if all(front == 0 for plane, partner, front in slots[0]) else []
    later = slot_jobs[len(early):]
    jobs = [[("diag", 0)] + early, [("diag", k) for k in range(1, fronts)] + later[:1]]
    jobs += [later[start:start + 2] for start in range(1, len(later), 2)]

    row_global = row_id * diag_rows + jnp.arange(diag_rows, dtype=jnp.int32)
    col_global = col_id * col_width + jnp.arange(col_width, dtype=jnp.int32)
    hit = row_global[:, None] == col_global[None, :]
    def diagonals(sums):
        base_diag = jnp.sum(jnp.where(hit, diag_inverse, 0.0), axis=1)
        cc_part = base_diag + sums.reshape(fronts, col_width)
        cc_near = cc_part
        bit = 1
        while bit < n_row:
            cc_near = cc_near + lax.ppermute(cc_near, "row", [(i, i ^ bit) for i in range(n_row)])
            bit *= 2
        cc_rows = lax.dynamic_slice_in_dim(cc_near, row_id % groups * diag_rows, diag_rows, 1)
        cc_far = cc_rows
        for shift in range(1, n_col):
            pairs = []
            for row in range(n_row):
                owner = row // groups
                pairs.append((row * n_col + owner, row * n_col + (owner + shift) % n_col))
            came = lax.ppermute(cc_rows, ("row", "col"), pairs)
            cc_far = jnp.where((col_id - row_id // groups) % n_col == shift, came, cc_far)
        return cc_near, cc_far

    diag_piece, direct, turned = {}, {}, {}
    cc_near, cc_far = diagonals(sums)
    picked = {}

    def side_of(at, after):
        if at not in picked:
            side = pick(col_id, {
                plane: got[partner < plane][spots[partner < plane][(front, partner)][plane]]
                for plane, partner, front in slots[at]
            }, after)
            picked[at] = (side, jnp.int32(0), lax.ppermute(side, "row", to_core), jnp.int32(0), 0)
        return picked[at]

    for number, job in enumerate(jobs):
        sides, which, used = [], [], []
        for kind, at in job:
            used += [at] if kind == "diag" else [front for plane, partner, front in slots[at]]
        used = sorted(set(used))
        for kind, at in job:
            if kind == "diag":
                sides.append((columns, row_id, columns, row_id ^ 1, at))
                which.append(jnp.int32(used.index(at)))
                continue
            sides.append(side_of(at, (halves[0],) if number > 1 else ()))
            front_of = {plane: used.index(front) for plane, partner, front in slots[at]}
            which.append(jnp.array([front_of.get(plane, 0) for plane in range(n_col)], jnp.int32)[col_id])
        after = (off,) + tuple(got[up][n_col] for up in got) if number == 0 else (cc_near, cc_far) if number == len(jobs) - 1 else ()
        halves = partial_blocks(sides, [(off, off_other, k) for k in used], which, row_id, col_width, groups, bits, after)
        for (kind, at), piece in zip(job, add_chips(halves, row_id, n_row, bits)):
            if kind == "diag":
                diag_piece[at] = piece
                continue
            sent = lax.ppermute(piece, "col", [(plane, partner) for plane, partner, front in slots[at]])
            sent = jnp.stack([
                jnp.concatenate([sent[h][:, g * diag_rows:(g + 1) * diag_rows] for h in range(groups)], axis=1)
                for g in range(groups)
            ])
            for plane, partner, front in slots[at]:
                direct[(plane, partner, front)] = piece
                turned[(partner, plane, front)] = sent
    z_far = lax.dynamic_slice_in_dim(z_diag[0], place, anc_rows, 0)

    is_child = edge_other < supercols
    at_col = edge_child[:, :, None] == col_global
    at_row = edge_other[:, :, None] == row_global
    at_anc = edge_other[:, :, None] == supercols + row_id * anc_rows + jnp.arange(anc_rows, dtype=jnp.int32)

    def picked(at, values):
        return jnp.sum(jnp.where(at, values, 0.0), axis=-1)

    def mixed_of(at, block):
        rows = jnp.einsum("ker,krc->kec", at.astype(jnp.float32), block, precision=lax.Precision.HIGHEST)
        return picked(at_col, rows)

    off_inverse = jnp.stack([off[:, k * col_width:(k + 1) * col_width] for k in range(fronts)])
    ends = picked(at_col, cc_near[:, None, :]) + picked(at_row, cc_far[:, None, :]) + picked(at_anc, z_far)
    ends = ends - 2.0 * mixed_of(at_anc, off_inverse)

    block_id = row_id // groups
    chunks = []
    straight = []
    for k in range(fronts):
        blocks = []
        for block in range(n_col):
            options = {}
            for plane in range(n_col):
                if plane == block:
                    options[plane] = diag_piece[k]
                elif (plane, block, k) in direct:
                    options[plane] = direct[(plane, block, k)]
                else:
                    options[plane] = turned[(plane, block, k)]
            blocks.append(choose(col_id, options))
        chunks.append(jnp.stack(blocks).reshape(n_row, -1, col_width))
        flag = jnp.zeros((), jnp.bool_)
        for plane in range(n_col):
            for block in range(n_col):
                if plane == block or (plane, block, k) in direct:
                    flag = jnp.logical_or(flag, jnp.logical_and(col_id == plane, block_id == block))
        straight.append(flag)
    chunks = jnp.stack(chunks, axis=1)
    found = lax.all_to_all(chunks, "row", 0, 0, tiled=True)
    diag_part = subtract_blocks(diag_inverse, found, jnp.stack(straight).astype(jnp.int32))
    resist = ends - 2.0 * mixed_of(at_row, diag_part)
    return (off_inverse, diag_part, resist)


def solution(mesh):
    placed = (
        P("row", "col"),
        P(None, "row", "col"),
        P(None, "row", "col"),
        P(None, "row"),
        P(None, ("row", "col")),
        P(None, ("row", "col")),
    )
    return jax.shard_map(
        per_device,
        mesh=mesh,
        in_specs=placed,
        out_specs=(P(None, "row", "col"), P(None, "row", "col"), P(None, ("row", "col"))),
        check_vma=False,
    )
```

```python
import functools

import jax
import jax.numpy as jnp
from jax import lax
from jax.experimental import pallas as pl
from jax.experimental.pallas import tpu as pltpu
from jax.sharding import PartitionSpec as P

SMALL = pl.CostEstimate(flops=0, bytes_accessed=0, transcendentals=0)


def assign_pairs(n_col, fronts):
    work = []
    for low in range(n_col):
        for high in range(low + 1, n_col):
            for front in range(fronts):
                middle = low + high - (n_col - 1)
                if high - low == 1:
                    middle = 0
                at_high = middle < 0 or (middle == 0 and front < fronts // 2)
                work.append((high, low, front) if at_high else (low, high, front))
    return work


def line_schedule(n_col, work, fronts, up):
    def fold(plane):
        return plane if up else n_col - 1 - plane

    wanted = {("z", src): n_col - 1 for src in range(n_col - 1)}
    for plane, partner, front in work:
        plane, partner = fold(plane), fold(partner)
        if partner < plane:
            wanted[(front, partner)] = max(wanted.get((front, partner), 0), plane)
    arrived = {key: {key[1]: 0} for key in wanted}
    rank = {"z": 0}
    for order, front in enumerate(range(fronts) if up else reversed(range(fronts))):
        rank[front] = 1 + order
    steps = []
    while True:
        sends = {}
        for plane in range(n_col - 1):
            ready = [
                key for key, last in wanted.items()
                if plane < last and plane in arrived[key] and plane + 1 not in arrived[key]
            ]
            if ready:
                sends[plane] = min(ready, key=lambda k: (k[0] != "z", -k[1] if k[0] == "z" else k[1], rank[k[0]]))
        if not sends:
            break
        steps.append(sends)
        for plane, key in sends.items():
            arrived[key][plane + 1] = len(steps)
    folded = [{fold(p): (k[0], fold(k[1])) for p, k in sends.items()} for sends in steps]
    where_at = {(k[0], fold(k[1])): {fold(p): s for p, s in at.items()} for k, at in arrived.items()}
    return folded, where_at


def color_slots(work, ready):
    slots = []
    load = [sum(it[0] == plane for it in work) for plane in range(1 + max(it[0] for it in work))]
    for item in sorted(work, key=lambda it: (ready[it], -load[it[0]], it)):
        for slot in slots:
            if all(other[0] != item[0] and other[1] != item[1] for other in slot):
                slot.append(item)
                break
        else:
            slots.append([item])
    return sorted(slots, key=lambda slot: max(ready[it] for it in slot))


def choose(index, options):
    groups = []
    for plane, array in options.items():
        for entry in groups:
            if entry[0] is array:
                entry[1].append(plane)
                break
        else:
            groups.append((array, [plane]))
    result = groups[0][0]
    for array, planes in groups[1:]:
        hit = index == planes[0]
        for plane in planes[1:]:
            hit = jnp.logical_or(hit, index == plane)
        result = jnp.where(hit, array, result)
    return result


def tie(value, after):
    return lax.optimization_barrier((value, after))[0]


def swap(part, axis, bit, n_row):
    mine = (lax.axis_index("row") >> bit) & 1
    send = lax.dynamic_index_in_dim(part, 1 - mine, axis, keepdims=False)
    keep = lax.dynamic_index_in_dim(part, mine, axis, keepdims=False)
    return keep + lax.ppermute(send, "row", [(i, i ^ (1 << bit)) for i in range(n_row)])


def reduce_scatter(halves, n_row, bits, after=None):
    other = [(i, i ^ 1) for i in range(n_row)]
    first = jnp.stack([kept + lax.ppermute(sent, "row", other) for kept, sent in halves])
    parts, groups, left_rows, rows, width = first.shape
    first = first.reshape((parts, groups) + (2,) * (bits - 1) + (rows, width))

    def run(piece, order):
        left = sorted(order, reverse=True)
        for bit in order:
            if after is not None and bit == order[-1]:
                piece = tie(piece, after)
            piece = swap(piece, 2 + left.index(bit), bit, n_row)
            left.remove(bit)
        return piece

    half = width // 2
    rest = list(range(1, bits))
    return first, jnp.concatenate([run(first[..., :half], rest), run(first[..., half:], rest[::-1])], axis=-1)


def split(value):
    upper = value.astype(jnp.bfloat16)
    return upper, (value - upper.astype(jnp.float32)).astype(jnp.bfloat16)


def three_pass(left, right, dims):
    (left_up, left_low), (right_up, right_low) = left, right
    dot = functools.partial(lax.dot_general, dimension_numbers=(dims, ((), ())), preferred_element_type=jnp.float32)
    return dot(left_up, right_up) + (dot(left_up, right_low) + dot(left_low, right_up))


def off_block(own, lower_blocks, upper_blocks, where, columns, factor):
    anc_rows, block = own.shape
    depth, width = columns.shape
    n_col = depth // block
    tile = min(256, width)

    def kernel(where, own_ref, *refs):
        lows, highs = refs[:n_col - 1], refs[n_col - 1:2 * n_col - 2]
        cols_ref, factor_ref, out_ref, sum_ref, diag_ref, upper, lower = refs[2 * n_col - 2:]
        hold, first = where[1], where[2]

        def take(shift, ref):
            upper[shift], lower[shift] = split(ref[...])

            @pl.when(lax.rem(where[0] - shift + n_col, n_col) == hold)
            def _():
                place = lax.broadcasted_iota(jnp.int32, ref.shape, 1) - lax.broadcasted_iota(jnp.int32, ref.shape, 0)
                diag_ref[...] = jnp.sum(jnp.where(place == first, ref[...], 0.0), axis=0, keepdims=True)

        @pl.when(pl.program_id(0) == 0)
        def _():
            take(0, own_ref)
            for shift in range(1, n_col):
                pl.when(where[0] >= shift)(functools.partial(take, shift, lows[shift - 1]))
                pl.when(where[0] < shift)(functools.partial(take, shift, highs[n_col - shift - 1]))

        total = jnp.zeros((anc_rows, tile), jnp.float32)
        for shift in range(n_col):
            at = lax.rem(where[0] - shift + n_col, n_col) * block
            right = split(cols_ref[pl.ds(pl.multiple_of(at, block), block), :])
            total -= three_pass((upper[shift], lower[shift]), right, ((1,), (0,)))
        out_ref[...] = total
        sum_ref[...] = -jnp.sum(total * factor_ref[...], axis=0, keepdims=True)

    whole = pl.BlockSpec((anc_rows, block), lambda n, where: (0, 0), pipeline_mode=pl.Buffered(1))
    return pl.pallas_call(
        kernel,
        grid_spec=pltpu.PrefetchScalarGridSpec(
            num_scalar_prefetch=1,
            grid=(width // tile,),
            in_specs=[whole] * (2 * n_col - 1) + [
                pl.BlockSpec((depth, tile), lambda n, where: (0, n)),
                pl.BlockSpec((anc_rows, tile), lambda n, where: (0, n)),
            ],
            out_specs=[
                pl.BlockSpec((anc_rows, tile), lambda n, where: (0, n)),
                pl.BlockSpec((1, tile), lambda n, where: (0, n)),
                pl.BlockSpec((1, block), lambda n, where: (0, 0)),
            ],
            scratch_shapes=[pltpu.VMEM((n_col, anc_rows, block), jnp.bfloat16)] * 2,
        ),
        out_shape=[
            jax.ShapeDtypeStruct((anc_rows, width), jnp.float32),
            jax.ShapeDtypeStruct((1, width), jnp.float32),
            jax.ShapeDtypeStruct((1, block), jnp.float32),
        ],
        compiler_params=pltpu.CompilerParams(vmem_limit_bytes=52 * 1024 * 1024),
        cost_estimate=pl.CostEstimate(
            flops=6 * anc_rows * depth * width, bytes_accessed=4 * (depth + 2 * anc_rows) * width, transcendentals=0
        ),
    )(where, own, *lower_blocks, *upper_blocks, columns, factor)


def partial_block(sides, which, off, front, mine, groups, bits, after=()):
    anc_rows, width = sides[0].shape
    tall = width // groups
    rows = tall >> bits

    def kernel(where, *refs):
        side_refs = refs[:len(sides)]
        off_ref = refs[len(sides)]
        kept_ref, sent_ref, upper, lower, side_up, side_low = refs[len(sides) + 1 + len(after):]

        @pl.when(pl.program_id(0) == 0)
        def _():
            upper[...], lower[...] = split(off_ref[...])

        def take(ref):
            side_up[...], side_low[...] = split(ref[...])

        for number, ref in enumerate(side_refs):
            pl.when(where[2] == number)(functools.partial(take, ref))
        found = three_pass((side_up[...], side_low[...]), (upper[...], lower[...]), ((0,), (0,)))
        found = found.reshape(1 << (bits - 1), 2, rows, width)
        zero = where[1] == 0
        kept_ref[0] = jnp.where(zero, found[:, 0], found[:, 1])
        sent_ref[0] = jnp.where(zero, found[:, 1], found[:, 0])

    out = jax.ShapeDtypeStruct((groups, 1 << (bits - 1), rows, width), jnp.float32)
    out_spec = pl.BlockSpec((1,) + out.shape[1:], lambda h, where: (h, 0, 0, 0))
    return pl.pallas_call(
        kernel,
        grid_spec=pltpu.PrefetchScalarGridSpec(
            num_scalar_prefetch=1,
            grid=(groups,),
            in_specs=[pl.BlockSpec((anc_rows, tall), lambda h, where: (0, h)) for _ in sides] + [
                pl.BlockSpec((anc_rows, width), lambda h, where: (0, where[0])),
            ] + [pl.BlockSpec(memory_space=pl.ANY) for _ in after],
            out_specs=[out_spec, out_spec],
            scratch_shapes=[pltpu.VMEM((anc_rows, width), jnp.bfloat16)] * 2
            + [pltpu.VMEM((anc_rows, tall), jnp.bfloat16)] * 2,
        ),
        out_shape=[out, out],
        compiler_params=pltpu.CompilerParams(vmem_limit_bytes=48 * 1024 * 1024),
        cost_estimate=SMALL,
    )(jnp.stack([front, mine, which]).astype(jnp.int32), *sides, off, *after)


def subtract_blocks(base, found, straight):
    fronts, tall, width = base.shape
    n_row, _, rows, _ = found.shape

    def kernel(flag, base_ref, found_ref, out_ref):
        block = found_ref[...].reshape(tall, tall)

        @pl.when(flag[pl.program_id(0)] == 1)
        def _():
            out_ref[0] = base_ref[0] - block

        @pl.when(flag[pl.program_id(0)] == 0)
        def _():
            out_ref[0] = base_ref[0] - block.T

    spec = pl.BlockSpec((1, tall, tall), lambda k, h, flag: (k, 0, h))
    return pl.pallas_call(
        kernel,
        grid_spec=pltpu.PrefetchScalarGridSpec(
            num_scalar_prefetch=1,
            grid=(fronts, width // tall),
            in_specs=[spec, pl.BlockSpec((n_row, 1, rows, tall), lambda k, h, flag: (0, k, 0, h))],
            out_specs=spec,
        ),
        out_shape=jax.ShapeDtypeStruct(base.shape, base.dtype),
        compiler_params=pltpu.CompilerParams(vmem_limit_bytes=32 * 1024 * 1024),
    )(straight, base, found)


def per_device(anc_inverse, off_factor, diag_inverse, block_mask, edge_child, edge_other):
    fronts, anc_rows, col_width = off_factor.shape
    diag_rows = diag_inverse.shape[1]
    anc_cols = anc_inverse.shape[1]
    row_id = lax.axis_index("row")
    col_id = lax.axis_index("col")
    n_row, n_col = lax.axis_size("row"), lax.axis_size("col")
    groups = col_width // diag_rows
    supercols, ancestor = col_width * n_col, anc_cols * n_col

    keep = jnp.repeat(block_mask, anc_rows // block_mask.shape[1], axis=1).astype(jnp.float32)
    factor = [off_factor[k] * keep[k][:, None] for k in range(fronts)]
    side_by_side = jnp.concatenate(factor, axis=1)
    columns = lax.all_gather(side_by_side, "row", axis=0, tiled=True)

    work = assign_pairs(n_col, fronts)
    plans = {up: line_schedule(n_col, work, fronts, up) for up in (True, False)}
    got = {up: {} for up in plans}
    spots = {up: plans[up][1] for up in plans}
    ready = {
        (plane, partner, front): spots[partner < plane][(front, partner)][plane] for plane, partner, front in work
    }

    def hop(number, after=()):
        earlier = tuple(got[up][number - 1] for up in got if number - 1 in got[up]) or (side_by_side,)
        operands = {}
        for up, (steps, where_at) in plans.items():
            if number > len(steps):
                continue
            options = {}
            for plane, (kind, src) in steps[number - 1].items():
                if src == plane:
                    options[plane] = anc_inverse if kind == "z" else factor[kind]
                else:
                    options[plane] = got[up][where_at[(kind, src)][plane]]
            operands[up] = choose(col_id, options)
        operands = tie(operands, earlier + tuple(after))
        for up, operand in operands.items():
            step = 1 if up else -1
            sends = sorted(plans[up][0][number - 1])
            got[up][number] = lax.ppermute(operand, "col", [(p, p + step) for p in sends])

    for number in range(1, n_col):
        hop(number)
    hop(n_col)
    steps_of = {up: [got[up][step] for step in range(1, n_col)] for up in got}
    owner = row_id * anc_rows // anc_cols
    place = row_id * anc_rows - owner * anc_cols
    off, minus_sums, z_diag = off_block(
        anc_inverse, steps_of[True], steps_of[False], jnp.stack([col_id, owner, place]), columns, side_by_side
    )
    z_far = lax.dynamic_slice_in_dim(z_diag[0], place, anc_rows, 0)
    last = max(len(steps) for steps, where_at in plans.values())
    for number in range(n_col + 1, last + 1):
        hop(number, (off,))

    row_global = row_id * diag_rows + jnp.arange(diag_rows, dtype=jnp.int32)
    col_global = col_id * col_width + jnp.arange(col_width, dtype=jnp.int32)
    hit = row_global[:, None] == col_global[None, :]
    base_diag = jnp.sum(jnp.where(hit, diag_inverse, 0.0), axis=1)
    cc_part = base_diag + minus_sums.reshape(fronts, col_width)
    cc_near = cc_part
    bit = 1
    while bit < n_row:
        cc_near = cc_near + lax.ppermute(cc_near, "row", [(i, i ^ bit) for i in range(n_row)])
        bit *= 2
    cc_rows = lax.dynamic_slice_in_dim(cc_near, row_id % groups * diag_rows, diag_rows, 1)
    cc_far = cc_rows
    for shift in range(1, n_col):
        pairs = []
        for row in range(n_row):
            owner = row // groups
            pairs.append((row * n_col + owner, row * n_col + (owner + shift) % n_col))
        came = lax.ppermute(cc_rows, ("row", "col"), pairs)
        cc_far = jnp.where((col_id - row_id // groups) % n_col == shift, came, cc_far)
    is_child = edge_other < supercols
    at_col = edge_child[:, :, None] == col_global
    at_row = edge_other[:, :, None] == row_global
    at_anc = edge_other[:, :, None] == supercols + row_id * anc_rows + jnp.arange(anc_rows, dtype=jnp.int32)

    def picked(at, values):
        return jnp.sum(jnp.where(at, values, 0.0), axis=-1)

    def mixed_of(at, block):
        rows = jnp.einsum("ker,krc->kec", at.astype(jnp.float32), block, precision=lax.Precision.HIGHEST)
        return picked(at_col, rows)

    off_inverse = jnp.stack([off[:, k * col_width:(k + 1) * col_width] for k in range(fronts)])
    ends = picked(at_col, cc_near[:, None, :]) + picked(at_row, cc_far[:, None, :]) + picked(at_anc, z_far)
    ends = ends - 2.0 * mixed_of(at_anc, off_inverse)

    bits = n_row.bit_length() - 1
    low_bit = row_id & 1
    slots = color_slots(work, ready)
    no = jnp.int32(0)
    if n_col in got[True]:
        off = tie(off, (got[True][n_col], got[False][n_col]))
    halves = [partial_block([factor[k]], no, off, jnp.int32(k), low_bit, groups, bits) for k in range(fronts)]
    first, pieces = reduce_scatter(halves, n_row, bits)
    diag_piece = list(pieces)
    for up in got:
        for step in got[up]:
            if step > n_col:
                got[up][step] = tie(got[up][step], pieces)
    direct, turned = {}, {}
    came = None
    for start in range(0, len(slots), 2):
        halves = []
        for slot in slots[start:start + 2]:
            sides, which, fronts_of = [], {}, {}
            for plane, partner, front in slot:
                side = got[partner < plane][spots[partner < plane][(front, partner)][plane]]
                if not any(side is known for known in sides):
                    sides.append(side)
                which[plane] = [side is known for known in sides].index(True)
                fronts_of[plane] = front
            if slot is slots[1]:
                sides = list(tie(tuple(sides), first))
            table = [jnp.array([of.get(plane, 0) for plane in range(n_col)], jnp.int32)[col_id] for of in (which, fronts_of)]
            newest = tuple(got[up][max(got[up])] for up in got)
            halves.append(partial_block(sides, table[0], off, table[1], low_bit, groups, bits, newest))
        pieces = reduce_scatter(halves, n_row, bits, came)[1]
        moved = []
        for slot, piece in zip(slots[start:start + 2], pieces):
            sent = lax.ppermute(piece, "col", [(plane, partner) for plane, partner, front in slot])
            moved.append(sent)
            sent = jnp.stack([
                jnp.concatenate([sent[h][:, g * diag_rows:(g + 1) * diag_rows] for h in range(groups)], axis=1)
                for g in range(groups)
            ])
            for plane, partner, front in slot:
                direct[(plane, partner, front)] = piece
                turned[(partner, plane, front)] = sent
        came = tuple(moved)

    block_id = row_id // groups
    chunks = []
    straight = []
    for k in range(fronts):
        blocks = []
        for block in range(n_col):
            options = {}
            for plane in range(n_col):
                if plane == block:
                    options[plane] = diag_piece[k]
                elif (plane, block, k) in direct:
                    options[plane] = direct[(plane, block, k)]
                else:
                    options[plane] = turned[(plane, block, k)]
            blocks.append(choose(col_id, options))
        chunks.append(jnp.stack(blocks).reshape(n_row, -1, col_width))
        flag = jnp.zeros((), jnp.bool_)
        for plane in range(n_col):
            for block in range(n_col):
                if plane == block or (plane, block, k) in direct:
                    flag = jnp.logical_or(flag, jnp.logical_and(col_id == plane, block_id == block))
        straight.append(flag)
    chunks = tie(jnp.stack(chunks, axis=1), ends)
    found = lax.all_to_all(chunks, "row", 0, 0, tiled=True)
    diag_part = subtract_blocks(diag_inverse, found, jnp.stack(straight).astype(jnp.int32))
    resist = ends - 2.0 * mixed_of(at_row, diag_part)
    return (off_inverse, diag_part, resist)


def solution(mesh):
    placed = (
        P("row", "col"),
        P(None, "row", "col"),
        P(None, "row", "col"),
        P(None, "row"),
        P(None, ("row", "col")),
        P(None, ("row", "col")),
    )
    return jax.shard_map(
        per_device,
        mesh=mesh,
        in_specs=placed,
        out_specs=(P(None, "row", "col"), P(None, "row", "col"), P(None, ("row", "col"))),
        check_vma=False,
    )
```
